32 devices in a mesh: groups: 2 (over x), rows: 8 (over z, y), query: 2 (over core).
Axes of the slice: x: 2, y: 2, z: 4, core: 2. Of those that a mesh axis runs over, the one named last changes fastest.
Arguments:
- activations: bfloat16 [1, 4096, 4096], P(None, ('groups', 'rows')), parts along dimension 1, may hold values from -52 to 52
- out_grads: bfloat16 [1, 4096, 4096], P(None, ('groups', 'rows')), parts along dimension 1, may hold values from -44 to 44
- proj_in: bfloat16 [1, 32, 4096], replicated, may hold values from -0.09375 to 0.09375
- proj_out: bfloat16 [1, 32, 4096], replicated, may hold values from -0.09375 to 0.09375
- queries: float32 [1, 2, 128, 1024], P(None, 'query', 'rows'), may hold values from -6 to 6
Outputs:
- scores: float32 [4096, 2, 128], P(('groups', 'rows'), 'query'), parts along dimension 0
The draws below stay inside these ranges and needn't reach their ends.
There are 2 independent parts, one for each index of `groups`. The reference program is written for one: setup_inputs(seed, part) draws one part's arguments, and reference() takes and returns one part's arrays. A program takes and returns all parts, laid end to end along the dimension named above; an argument that names none is the same for every part. Nothing has to cross between parts.
All inputs are finite; a program needn't handle non-finite values.
Results may differ from the reference program's by a relative error of at most 0.0003.
Values sent between devices are 32-bit elements; how exact they have to be, the bound alone decides.
A program may use at most 128 MiB of HBM per device.

```python
import jax
import jax.numpy as jnp
from jax import lax

D = 4096
PI = 32
PO = 32
L = 1
K = 1024
TOTAL = 2048
NQH = 128
NQS = 2


cluster_count = 16


def shared_layout(key):
    key_member, key_balance, key_level = jax.random.split(key, 3)
    member = jax.random.randint(key_member, (L, TOTAL), 0, cluster_count)
    balance = jax.random.uniform(key_balance, (L, cluster_count), jnp.float32, -1.9, 1.9)
    row_level = jax.random.uniform(key_level, (L, TOTAL, 1), jnp.float32, -1.0, 1.0)
    return (member, balance, row_level)


def pick_rows(table, member):
    return table[member]


def shape_field(key, noise, member, balance, row_level, orient, spread):
    key_dirs, key_jitter = jax.random.split(key)
    directions = jnp.clip(jax.random.normal(key_dirs, (L, cluster_count, D), jnp.float32), -2.0, 2.0)
    jitter = jax.random.uniform(key_jitter, (L, cluster_count), jnp.float32, -0.35, 0.35)
    magnitude = jnp.exp(orient * balance + jitter)
    means = jax.vmap(pick_rows)(directions * magnitude[:, :, None], member)
    scale = jnp.exp(spread * row_level)
    return (scale * (noise + means)).astype(jnp.bfloat16)


def draw_activations(key, part):
    member, balance, row_level = shared_layout(key)
    key = jax.random.fold_in(key, 11)
    key_noise, key_rest = jax.random.split(key)
    noise = jnp.clip(jax.random.normal(key_noise, (L, TOTAL, D), jnp.float32), -4.0, 4.0)
    return shape_field(key_rest, noise, member, balance, row_level, -1.0, 0.55)


def draw_out_grads(key, part):
    member, balance, row_level = shared_layout(key)
    key = jax.random.fold_in(key, 23)
    key_noise, key_rest = jax.random.split(key)
    noise = jnp.clip(jax.random.normal(key_noise, (L, TOTAL, D), jnp.float32), -4.0, 4.0)
    return shape_field(key_rest, noise, member, balance, row_level, 1.0, 0.4)


def steps_of(own_key, extent, pieces, smallest, largest):
    level, own = 1.0, jax.random.fold_in(own_key, 6)
    for dim, parts in pieces:
        draws = jnp.exp(jax.random.uniform(jax.random.fold_in(own, dim), (parts,), jnp.float32, smallest / len(pieces), largest / len(pieces)))
        level = level * jnp.repeat(draws, extent[dim] // parts).reshape([-1 if axis == dim else 1 for axis in range(len(extent))])
    return level


def centred(rng, shape, scale, bound, cuts=(), kind=jnp.bfloat16):
    level = steps_of(rng, shape, cuts, -0.22, 0.18) if cuts else 1.0
    result = jax.random.normal(rng, shape, jnp.float32) * scale * level
    return jnp.minimum(jnp.maximum(result, -bound), bound).astype(kind)


def setup_inputs(seed: int = 0, part: int = 0) -> dict:
    seeds = jax.random.split(jax.random.key(seed), 6)
    part_splits = jax.random.split(jax.random.fold_in(seeds[5], part), 6)
    return {
        "activations": draw_activations(jax.random.fold_in(jax.random.fold_in(seeds[5], part), 71), part),
        "out_grads": draw_out_grads(jax.random.fold_in(jax.random.fold_in(seeds[5], part), 71), part),
        "proj_in": centred(seeds[2], (L, PI, D), D ** -0.5, 0.09375),
        "proj_out": centred(seeds[3], (L, PO, D), D ** -0.5, 0.09375),
        "queries": centred(seeds[4], (L, NQS, NQH, K), 1.0, 6.0, ((1, 2), (2, 8)), jnp.float32),
    }


def precondition(chol, rhs):
    lower = lax.linalg.triangular_solve(chol, rhs, left_side=True, lower=True)
    return lax.linalg.triangular_solve(chol, lower, left_side=True, lower=True, transpose_a=True)

def reference(activations, out_grads, proj_in, proj_out, queries):
    hp = lax.Precision.HIGHEST
    total = jnp.zeros((TOTAL, NQS * NQH), jnp.float32)
    for layer in range(L):
        xs = jnp.dot(activations[layer].astype(jnp.float32), proj_in[layer].T.astype(jnp.float32), preferred_element_type=jnp.float32)
        gs = jnp.dot(out_grads[layer].astype(jnp.float32), proj_out[layer].T.astype(jnp.float32), preferred_element_type=jnp.float32)
        sketch = (gs[:, :, None] * xs[:, None, :]).reshape(TOTAL, K)
        fisher = jnp.dot(sketch.T, sketch, precision=hp) / TOTAL
        damp = 0.1 * jnp.trace(fisher) / K
        system = fisher + damp * jnp.eye(K, dtype=jnp.float32)
        chol = jnp.linalg.cholesky(system)
        flat = queries[layer].reshape(NQS * NQH, K)
        solved = precondition(chol, flat.T)
        total = total + jnp.dot(sketch, solved, precision=hp)
    return (total / jnp.sqrt(jnp.float32(K))).reshape(TOTAL, NQS, NQH)
```

```python
import functools

import jax
import jax.numpy as jnp
from jax import lax
from jax.experimental import pallas as pl
from jax.experimental.pallas import tpu as pltpu
from jax.sharding import PartitionSpec as P

BLOCK = 128
SUB = 8
MOST_PARTS = 8


def split(a):
    high = a.astype(jnp.bfloat16)
    low = (a - high.astype(jnp.float32)).astype(jnp.bfloat16)
    return high, low


def product(a, b, contract):
    (ah, al), (bh, bl) = a, b
    dims = (contract, ((), ()))
    dot = functools.partial(lax.dot_general, dimension_numbers=dims, preferred_element_type=jnp.float32)
    return dot(ah, bh) + (dot(ah, bl) + dot(al, bh))


def spread(a, shape):
    return lax.broadcast_in_dim(a, shape, (0, 1))


def invert(a):
    size = a.shape[0]
    shape = (SUB, size)
    rows = [a[s * SUB : (s + 1) * SUB] for s in range(size // SUB)]
    lane = lax.broadcasted_iota(jnp.int32, shape, 1)
    sub = lax.broadcasted_iota(jnp.int32, shape, 0)
    for p in range(len(rows)):
        at = p * SUB
        inside = (lane >= at) & (lane < at + SUB)
        own = rows[p]
        cols = [spread(own[:, at + j : at + j + 1], shape) for j in range(SUB)]
        own = jnp.where(inside, jnp.where(lane - at == sub, 1.0, 0.0), own)
        for j in range(SUB):
            inverse = 1.0 / spread(cols[j][j : j + 1], shape)
            here = sub == j
            for i in range(j + 1, SUB):
                scaled = spread(cols[i][j : j + 1], shape) * inverse
                cols[i] = jnp.where(here, scaled, cols[i] - cols[j] * scaled)
            scaled = spread(own[j : j + 1], shape) * inverse
            own = jnp.where(here, scaled, own - cols[j] * scaled)
        pivots = [spread(own[j : j + 1], shape) for j in range(SUB)]
        for s in range(len(rows)):
            if s == p:
                continue
            terms = [spread(rows[s][:, at + j : at + j + 1], shape) * pivots[j] for j in range(SUB)]
            while len(terms) > 1:
                terms = [x + y for x, y in zip(terms[::2], terms[1::2])]
            rows[s] = jnp.where(inside, 0.0, rows[s]) - terms[0]
        rows[p] = own
    return jnp.concatenate(rows, axis=0)


def score_kernel(own_ref, all_ref, queries_ref, out_ref, high, low, work, mat):
    parts, both, local_rows = all_ref.shape
    width, total = work.shape
    queries = queries_ref.shape[0]
    half = both // 2
    all_rows = parts * local_rows
    group = high.shape[1] // local_rows
    wide = min(2 * BLOCK, width)

    for o in range(half):
        work[o * half : (o + 1) * half, width : width + local_rows] = own_ref[half + o : half + o + 1, :] * own_ref[:half, :]
    for c in range(0, width, BLOCK):
        work[c : c + BLOCK, width + local_rows :] = queries_ref[:, c : c + BLOCK].T

    def gather_group(first, start):
        def fill(part, carry):
            xs = all_ref[first + part, :half, :]
            gs = all_ref[first + part, half:, :]
            columns = pl.ds(pl.multiple_of(part * local_rows, local_rows), local_rows)
            for o in range(half):
                h, l = split(gs[o : o + 1, :] * xs)
                high[o * half : (o + 1) * half, columns] = h
                low[o * half : (o + 1) * half, columns] = l
            return carry

        lax.fori_loop(0, group, fill, 0)
        for i in range(0, width, wide):
            block = product((high[i : i + wide, :], low[i : i + wide, :]), (high[i:, :], low[i:, :]), ((1,), (1,)))
            if start:
                work[i : i + wide, i:width] = block
            else:
                work[i : i + wide, i:width] += block

    gather_group(0, True)
    if parts > group:

        @pl.loop(1, parts // group)
        def _(step):
            gather_group(step * group, False)

    eye = lax.broadcasted_iota(jnp.int32, (BLOCK, BLOCK), 0) == lax.broadcasted_iota(jnp.int32, (BLOCK, BLOCK), 1)
    diagonal = jnp.zeros((BLOCK, BLOCK), jnp.float32)
    for c in range(0, width, BLOCK):
        diagonal += jnp.where(eye, work[c : c + BLOCK, c : c + BLOCK], 0.0)
    damp = jnp.where(eye, 0.1 / width * jnp.sum(diagonal), 0.0)
    for c in range(0, width, BLOCK):
        work[c : c + BLOCK, c : c + BLOCK] += damp

    for k in range(0, width, BLOCK):
        after = k + BLOCK
        inverse = invert(work[k : k + BLOCK, k : k + BLOCK])
        mat[:, after:] = product(split(inverse), split(work[k : k + BLOCK, after:]), ((1,), (0,)))
        for i in range(after, width, BLOCK):
            left = split(work[k : k + BLOCK, i : i + BLOCK].T)
            work[i : i + BLOCK, i:] -= product(left, split(mat[:, i:]), ((1,), (0,)))
        left = split(work[k : k + BLOCK, width : width + local_rows].T)
        term = product(left, split(mat[:, width + local_rows :]), ((1,), (0,)))
        if k == 0:
            out_ref[...] = term
        else:
            out_ref[...] += term
    out_ref[...] *= all_rows / width**0.5


def scores_of(own, everyone, queries):
    parts, both, local_rows = everyone.shape
    count, width = queries.shape
    group = min(parts, MOST_PARTS)
    assert parts % group == 0 and width == (both // 2) ** 2
    total = width + local_rows + count
    return pl.pallas_call(
        score_kernel,
        out_shape=jax.ShapeDtypeStruct((local_rows, count), jnp.float32),
        in_specs=[pl.BlockSpec(memory_space=pltpu.VMEM)] * 3,
        out_specs=pl.BlockSpec(memory_space=pltpu.VMEM),
        scratch_shapes=[
            pltpu.VMEM((width, group * local_rows), jnp.bfloat16),
            pltpu.VMEM((width, group * local_rows), jnp.bfloat16),
            pltpu.VMEM((width, total), jnp.float32),
            pltpu.VMEM((BLOCK, total), jnp.float32),
        ],
        compiler_params=pltpu.CompilerParams(vmem_limit_bytes=56 * 2**20),
        name="scores",
    )(own, everyone, queries)


def project(projector, values):
    return lax.dot_general(projector, values, (((1,), (1,)), ((), ())), preferred_element_type=jnp.float32)


def body(activations, out_grads, proj_in, proj_out, queries):
    everyone_queries = lax.all_gather(queries[0, 0], "rows", axis=0, tiled=True)
    own = jnp.concatenate([project(proj_in[0], activations[0]), project(proj_out[0], out_grads[0])], axis=0)
    everyone = lax.all_gather(own, "rows", axis=0)
    result = scores_of(own, everyone, everyone_queries)
    return result.reshape(result.shape[0], 1, result.shape[1])


def solution(mesh):
    return jax.shard_map(
        body,
        mesh=mesh,
        in_specs=(
            P(None, ("groups", "rows"), None),
            P(None, ("groups", "rows"), None),
            P(),
            P(),
            P(None, "query", "rows", None),
        ),
        out_specs=P(("groups", "rows"), "query", None),
        check_vma=False,
    )
```

```python
import functools

import jax
import jax.numpy as jnp
from jax import lax
from jax.experimental import pallas as pl
from jax.experimental.pallas import tpu as pltpu
from jax.sharding import PartitionSpec as P

BLOCK = 128
SUB = 8
MOST_PARTS = 8


def split(a):
    high = a.astype(jnp.bfloat16)
    low = (a - high.astype(jnp.float32)).astype(jnp.bfloat16)
    return high, low


def product(a, b, contract):
    (ah, al), (bh, bl) = a, b
    dims = (contract, ((), ()))
    dot = functools.partial(lax.dot_general, dimension_numbers=dims, preferred_element_type=jnp.float32)
    return dot(ah, bh) + (dot(ah, bl) + dot(al, bh))


def spread(a, shape):
    return lax.broadcast_in_dim(a, shape, (0, 1))


def invert(a):
    size = a.shape[0]
    shape = (SUB, size)
    rows = [a[s * SUB : (s + 1) * SUB] for s in range(size // SUB)]
    lane = lax.broadcasted_iota(jnp.int32, shape, 1)
    sub = lax.broadcasted_iota(jnp.int32, shape, 0)
    for p in range(len(rows)):
        at = p * SUB
        inside = (lane >= at) & (lane < at + SUB)
        own = rows[p]
        cols = [spread(own[:, at + j : at + j + 1], shape) for j in range(SUB)]
        own = jnp.where(inside, jnp.where(lane - at == sub, 1.0, 0.0), own)
        for j in range(SUB):
            inverse = 1.0 / spread(cols[j][j : j + 1], shape)
            here = sub == j
            for i in range(j + 1, SUB):
                scaled = spread(cols[i][j : j + 1], shape) * inverse
                cols[i] = jnp.where(here, scaled, cols[i] - cols[j] * scaled)
            scaled = spread(own[j : j + 1], shape) * inverse
            own = jnp.where(here, scaled, own - cols[j] * scaled)
        pivots = [spread(own[j : j + 1], shape) for j in range(SUB)]
        for s in range(len(rows)):
            if s == p:
                continue
            terms = [spread(rows[s][:, at + j : at + j + 1], shape) * pivots[j] for j in range(SUB)]
            while len(terms) > 1:
                terms = [x + y for x, y in zip(terms[::2], terms[1::2])]
            rows[s] = jnp.where(inside, 0.0, rows[s]) - terms[0]
        rows[p] = own
    return jnp.concatenate(rows, axis=0)


def score_kernel(own_ref, all_ref, queries_ref, out_ref, high, low, work, mat):
    parts, both, local_rows = all_ref.shape
    width, total = work.shape
    queries = queries_ref.shape[0]
    half = both // 2
    all_rows = parts * local_rows
    group = high.shape[1] // local_rows
    wide = min(2 * BLOCK, width)

    for o in range(half):
        work[o * half : (o + 1) * half, width : width + local_rows] = own_ref[half + o : half + o + 1, :] * own_ref[:half, :]
    for c in range(0, width, BLOCK):
        work[c : c + BLOCK, width + local_rows :] = queries_ref[:, c : c + BLOCK].T

    def gather_group(first, start):
        def fill(part, carry):
            xs = all_ref[first + part, :half, :]
            gs = all_ref[first + part, half:, :]
            columns = pl.ds(pl.multiple_of(part * local_rows, local_rows), local_rows)
            for o in range(half):
                h, l = split(gs[o : o + 1, :] * xs)
                high[o * half : (o + 1) * half, columns] = h
                low[o * half : (o + 1) * half, columns] = l
            return carry

        lax.fori_loop(0, group, fill, 0)
        for i in range(0, width, wide):
            block = product((high[i : i + wide, :], low[i : i + wide, :]), (high[i:, :], low[i:, :]), ((1,), (1,)))
            if start:
                work[i : i + wide, i:width] = block
            else:
                work[i : i + wide, i:width] += block

    gather_group(0, True)
    if parts > group:

        @pl.loop(1, parts // group)
        def _(step):
            gather_group(step * group, False)

    eye = lax.broadcasted_iota(jnp.int32, (BLOCK, BLOCK), 0) == lax.broadcasted_iota(jnp.int32, (BLOCK, BLOCK), 1)
    diagonal = jnp.zeros((BLOCK, BLOCK), jnp.float32)
    for c in range(0, width, BLOCK):
        diagonal += jnp.where(eye, work[c : c + BLOCK, c : c + BLOCK], 0.0)
    damp = jnp.where(eye, 0.1 / width * jnp.sum(diagonal), 0.0)
    for c in range(0, width, BLOCK):
        work[c : c + BLOCK, c : c + BLOCK] += damp

    for k in range(0, width, BLOCK):
        after = k + BLOCK
        inverse = invert(work[k : k + BLOCK, k : k + BLOCK])
        mat[:, after:] = product(split(inverse), split(work[k : k + BLOCK, after:]), ((1,), (0,)))
        for i in range(after, width, BLOCK):
            left = split(work[k : k + BLOCK, i : i + BLOCK].T)
            work[i : i + BLOCK, i:] -= product(left, split(mat[:, i:]), ((1,), (0,)))
        left = split(work[k : k + BLOCK, width : width + local_rows].T)
        term = product(left, split(mat[:, width + local_rows :]), ((1,), (0,)))
        if k == 0:
            out_ref[...] = term
        else:
            out_ref[...] += term
    out_ref[...] *= all_rows / width**0.5


def scores_of(own, everyone, queries):
    parts, both, local_rows = everyone.shape
    count, width = queries.shape
    group = min(parts, MOST_PARTS)
    assert parts % group == 0 and width == (both // 2) ** 2
    total = width + local_rows + count
    return pl.pallas_call(
        score_kernel,
        out_shape=jax.ShapeDtypeStruct((local_rows, count), jnp.float32),
        in_specs=[pl.BlockSpec(memory_space=pltpu.VMEM)] * 3,
        out_specs=pl.BlockSpec(memory_space=pltpu.VMEM),
        scratch_shapes=[
            pltpu.VMEM((width, group * local_rows), jnp.bfloat16),
            pltpu.VMEM((width, group * local_rows), jnp.bfloat16),
            pltpu.VMEM((width, total), jnp.float32),
            pltpu.VMEM((BLOCK, total), jnp.float32),
        ],
        compiler_params=pltpu.CompilerParams(vmem_limit_bytes=56 * 2**20),
        name="scores",
    )(own, everyone, queries)


def gather_kernel(own_ref, part_ref, all_ref, queries_ref, send, recv):
    parts = all_ref.shape[0]
    me = lax.axis_index("rows")
    peers = [lax.rem(me + step, parts) for step in range(1, parts)]
    barrier = pltpu.get_barrier_semaphore()
    for peer in peers:
        pl.semaphore_signal(barrier, inc=1, device_id={"rows": peer}, device_id_type=pl.DeviceIdType.MESH)
    pl.semaphore_wait(barrier, parts - 1)
    copies = []
    for step, peer in enumerate(peers):
        for which, (source, target) in enumerate(((own_ref, all_ref), (part_ref, queries_ref))):
            copy = pltpu.make_async_remote_copy(
                src_ref=source,
                dst_ref=target.at[me],
                send_sem=send.at[which, step],
                recv_sem=recv.at[which, step],
                device_id={"rows": peer},
                device_id_type=pl.DeviceIdType.MESH,
            )
            copy.start()
            copies.append(copy)
    all_ref[me] = own_ref[...]
    queries_ref[me] = part_ref[...]
    for copy in copies:
        copy.wait()


def gather_both(own, part):
    parts = lax.axis_size("rows")
    return pl.pallas_call(
        gather_kernel,
        out_shape=[
            jax.ShapeDtypeStruct((parts, *own.shape), jnp.float32),
            jax.ShapeDtypeStruct((parts, *part.shape), jnp.float32),
        ],
        in_specs=[pl.BlockSpec(memory_space=pltpu.VMEM)] * 2,
        out_specs=[pl.BlockSpec(memory_space=pltpu.VMEM)] * 2,
        scratch_shapes=[pltpu.SemaphoreType.DMA((2, parts - 1)), pltpu.SemaphoreType.DMA((2, parts - 1))],
        compiler_params=pltpu.CompilerParams(collective_id=0, has_side_effects=True, vmem_limit_bytes=40 * 2**20),
        name="gather",
    )(own, part)


def project(projector, values):
    return lax.dot_general(projector, values, (((1,), (1,)), ((), ())), preferred_element_type=jnp.float32)


def body(activations, out_grads, proj_in, proj_out, queries):
    own = jnp.concatenate([project(proj_in[0], activations[0]), project(proj_out[0], out_grads[0])], axis=0)
    everyone, everyone_queries = gather_both(own, queries[0, 0])
    result = scores_of(own, everyone, everyone_queries.reshape(-1, queries.shape[3]))
    return result.reshape(result.shape[0], 1, result.shape[1])


def solution(mesh):
    return jax.shard_map(
        body,
        mesh=mesh,
        in_specs=(
            P(None, ("groups", "rows"), None),
            P(None, ("groups", "rows"), None),
            P(),
            P(),
            P(None, "query", "rows", None),
        ),
        out_specs=P(("groups", "rows"), "query", None),
        check_vma=False,
    )
```
